32 devices in a mesh: dp: 4 (over y, core), expert: 8 (over z, x).
Axes of the slice: x: 2, y: 2, z: 4, core: 2. Of those that a mesh axis runs over, the one named last changes fastest.
Arguments:
- tokens: bfloat16 [4096, 1024], P(('dp', 'expert')), may hold values from -6 to 6
- cotangent: bfloat16 [4096, 1024], P(('dp', 'expert')), may hold values from -0.75 to 0.75
- routes: int32 [4096, 8], P(('dp', 'expert')), may hold values from 0 to 15, all different within a row; in each aligned block of 128 rows (0 to 127, 128 to 255, ...) at most 128 rows name the same one
- route_weight: bfloat16 [4096, 8], P(('dp', 'expert')), may hold values from 0.049804688 to 1
- w_gate: bfloat16 [16, 1024, 384], P('expert'), may hold values from -0.1875 to 0.1875
- w_up: bfloat16 [16, 1024, 384], P('expert'), may hold values from -0.1875 to 0.1875
- w_down: bfloat16 [16, 1024, 384], P('expert'), may hold values from -0.3125 to 0.3125
Outputs:
- grad_tokens: bfloat16 [4096, 1024], P(('dp', 'expert'))
- grad_route_weight: bfloat16 [4096, 8], P(('dp', 'expert'))
- grad_w_gate: bfloat16 [16, 1024, 384], P('expert', 'dp')
- grad_w_up: bfloat16 [16, 1024, 384], P('expert', 'dp')
- grad_w_down: bfloat16 [16, 1024, 384], P('expert', 'dp')
The draws below stay inside these ranges and needn't reach their ends.
Inputs may be any that keep to these rules, and one draw needn't show every extreme that they name: `routes`: in the 128 rows of one device no expert is named by more than 128 rows, and in some devices' rows one expert is named by exactly 128 rows.
All inputs are finite; a program needn't handle non-finite values.
Results may differ from the reference program's by a relative error of at most 0.012.
Values may be sent and summed in bfloat16 or wider, within the bound.
A program may use at most 128 MiB of HBM per device.

```python
import math
import jax
import jax.numpy as jnp
import numpy as np
from jax import lax

D = 1024
FF = 384
TOPK = 8
TOK_DEV = 128
EXPERTS = 16
CAP = 128
TOKENS = 4096
N_DP = 4
N_EXPERT = 8


def level_of(stream_key, shape, split, smallest, high):
    def one(position, blocks):
        draws = jax.random.uniform(jax.random.fold_in(jax.random.fold_in(stream_key, 6), position), (blocks,), jnp.float32, smallest / len(split), high / len(split))
        return jnp.repeat(jnp.exp(draws), shape[position] // blocks).reshape((-1,) + (1,) * (len(shape) - position - 1))

    level = one(*split[0])
    for cut in split[1:]:
        level = level * one(*cut)
    return level


def assign_block(rng, own, number, rows, number_of, top, most, slope):
    ranking = jax.random.permutation(rng, number_of)
    packed, usual = portions_of(number_of, rows * top, most, slope, True), portions_of(number_of, rows * top, most, slope, False)
    places = jnp.arange(number_of)

    def named(sizes, offset_by):
        used = int((sizes > 0).sum())
        fixed = max(1, used // 4)
        passed = fixed + (places - fixed + offset_by * (used - fixed)) % max(1, number_of - fixed)
        return jnp.zeros((number_of,), jnp.int32).at[ranking[jnp.where(places < fixed, places, passed)]].set(jnp.asarray(sizes, jnp.int32))

    sizes = jnp.where(number % 4 == 0, named(packed, number // 4), named(usual, number - number // 4 - 1))
    mixed = jax.random.permutation(jax.random.fold_in(own, 3), number_of)
    donor, taker = mixed[0:number_of // 2 * 2:2], mixed[1:number_of // 2 * 2:2]
    slack = jnp.minimum(sizes[donor] - 1, most - sizes[taker]) // 2
    slack = jnp.where((donor == ranking[0]) | (taker == ranking[0]) | (sizes[taker] == 0), 0, jnp.maximum(slack, 0))
    passed = jax.random.randint(jax.random.fold_in(own, 4), (number_of // 2,), 0, 1 << 20) % (slack + 1)
    sizes = sizes.at[donor].add(-passed).at[taker].add(passed)
    items = jnp.searchsorted(jnp.cumsum(sizes), jnp.arange(rows * top), side="right").astype(jnp.int32)
    grid = items.reshape(top, rows).T
    grid = grid[jax.random.permutation(jax.random.fold_in(own, 1), rows)]
    offset_by = jax.random.randint(jax.random.fold_in(own, 2), (rows, 1), 0, top)
    return jnp.take_along_axis(grid, (jnp.arange(top)[None, :] + offset_by) % top, axis=1)


def portions_of(number_of, total, most, skew, full):
    weights = [(1 << 20) // math.isqrt(grade ** skew) + 1 for grade in range(1, number_of + 1)]
    largest = most if full else min(most, max(-(-total // number_of), total * weights[0] // sum(weights)))
    least = 1 if total - largest >= number_of - 1 else 0
    given, spare = [largest] + [least] * (number_of - 1), total - largest - least * (number_of - 1)
    while spare > 0:
        free = [i for i in range(1, number_of) if given[i] < largest] or [i for i in range(1, number_of) if given[i] < most]
        pool, remaining = sum([weights[i] for i in free]), spare
        for i in free:
            extra = min(most - given[i], max(1, remaining * weights[i] // pool), spare)
            given[i] = given[i] + extra
            spare = spare - extra
    return np.array(given)


def bell_draw(rng, dims, scale, reach, pieces=(), kind=jnp.bfloat16):
    result = jax.random.normal(rng, dims, jnp.float32) * scale
    if len(pieces) > 0:
        result = level_of(rng, dims, pieces, -0.22, 0.18) * result
    return jnp.clip(result, min=-reach, max=reach).astype(kind)


def setup_inputs(seed: int = 0) -> dict:
    keys = jax.random.split(jax.random.key(seed), 8)
    tokens = bell_draw(keys[0], (TOKENS, D), 1.0, 6.0, ((0, 32),))
    cotangent = bell_draw(keys[1], (TOKENS, D), 0.125, 0.75, ((0, 32),))
    routes_keys = jax.random.split(jax.random.fold_in(keys[2], 1), TOKENS // TOK_DEV)
    routes_turns = jax.random.permutation(jax.random.fold_in(keys[2], 3), TOKENS // TOK_DEV)
    routes = jax.vmap(lambda own, number: assign_block(jax.random.fold_in(keys[2], 2), own, number, TOK_DEV, EXPERTS, TOPK, CAP, 2))(routes_keys, routes_turns).reshape((TOKENS, TOPK))
    route_weight = jnp.clip(jnp.exp(math.log(1.0) - 2.9996462 * jax.random.uniform(keys[3], (TOKENS, TOPK), jnp.float32) ** level_of(keys[3], (TOKENS, TOPK), ((0, 32),), -0.2, 0.2)), 0.049804688, 1.0).astype(jnp.bfloat16)
    w_gate = bell_draw(keys[4], (EXPERTS, D, FF), D ** -0.5, 0.1875, ((0, 8),))
    w_up = bell_draw(keys[5], (EXPERTS, D, FF), D ** -0.5, 0.1875, ((0, 8),))
    w_down = bell_draw(keys[6], (EXPERTS, D, FF), FF ** -0.5, 0.3125, ((0, 8),))
    return {"tokens": tokens, "cotangent": cotangent, "routes": routes, "route_weight": route_weight, "w_gate": w_gate, "w_up": w_up, "w_down": w_down}


def expert_rows(x_rows, g_rows, w_rows, gate_w, up_w, down_w):
    gate_act = jnp.dot(x_rows, gate_w, preferred_element_type=jnp.float32)
    up_act = jnp.dot(x_rows, up_w, preferred_element_type=jnp.float32)
    sigmoid_gate = jax.nn.sigmoid(gate_act)
    silu_gate = gate_act * sigmoid_gate
    hidden = (silu_gate * up_act).astype(jnp.bfloat16)
    expert_out = jnp.dot(hidden, down_w.T, preferred_element_type=jnp.float32)
    row_score = jnp.sum(expert_out * g_rows.astype(jnp.float32), axis=-1).astype(jnp.bfloat16)
    grad_out = (w_rows.astype(jnp.float32)[:, None] * g_rows.astype(jnp.float32)).astype(jnp.bfloat16)
    grad_hidden = jnp.dot(grad_out, down_w, preferred_element_type=jnp.float32)
    deriv = sigmoid_gate * (1.0 + gate_act * (1.0 - sigmoid_gate))
    grad_gate = (grad_hidden * up_act * deriv).astype(jnp.bfloat16)
    grad_up = (grad_hidden * silu_gate).astype(jnp.bfloat16)
    grad_rows = (jnp.dot(grad_gate, gate_w.T, preferred_element_type=jnp.float32)
                 + jnp.dot(grad_up, up_w.T, preferred_element_type=jnp.float32)).astype(jnp.bfloat16)
    grad_gate_w = jnp.dot(x_rows.T, grad_gate, preferred_element_type=jnp.float32)
    grad_up_w = jnp.dot(x_rows.T, grad_up, preferred_element_type=jnp.float32)
    grad_down_w = jnp.dot(grad_out.T, hidden, preferred_element_type=jnp.float32)
    return grad_rows, row_score, grad_gate_w, grad_up_w, grad_down_w


def reference(tokens, cotangent, routes, route_weight, w_gate, w_up, w_down):
    token_count = tokens.shape[0]
    top_count = routes.shape[1]
    route_count = token_count * top_count
    flat_routes = routes.reshape(-1).astype(jnp.int32)
    sorted_ids = jnp.argsort(flat_routes, stable=True).astype(jnp.int32)
    counts = jnp.zeros((EXPERTS,), jnp.int32).at[flat_routes].add(1)
    starts = (jnp.cumsum(counts) - counts).astype(jnp.int32)
    max_rows = N_DP * N_EXPERT * CAP
    padded_ids = jnp.concatenate([sorted_ids, jnp.zeros((max_rows,), jnp.int32)])
    flat_weight = route_weight.reshape(-1)

    def per_expert(state_pair, expert):
        grad_acc, score_acc = state_pair
        slice_ids = lax.dynamic_slice(padded_ids, (starts[expert],), (max_rows,))
        is_valid = jnp.arange(max_rows, dtype=jnp.int32) < counts[expert]
        route_ids = jnp.where(is_valid, slice_ids, route_count).astype(jnp.int32)
        token_ids = jnp.where(is_valid, slice_ids // top_count, token_count).astype(jnp.int32)
        x_rows = jnp.take(tokens, token_ids, axis=0, mode="fill", fill_value=0)
        g_rows = jnp.take(cotangent, token_ids, axis=0, mode="fill", fill_value=0)
        w_rows = jnp.take(flat_weight, route_ids, axis=0, mode="fill", fill_value=0)
        gate_w = lax.dynamic_index_in_dim(w_gate, expert, 0, keepdims=False)
        up_w = lax.dynamic_index_in_dim(w_up, expert, 0, keepdims=False)
        down_w = lax.dynamic_index_in_dim(w_down, expert, 0, keepdims=False)
        grad_rows, row_score, grad_gate_w, grad_up_w, grad_down_w = expert_rows(
            x_rows, g_rows, w_rows, gate_w, up_w, down_w)
        grad_acc = grad_acc.at[token_ids].add(grad_rows.astype(jnp.float32), mode="drop")
        score_acc = score_acc.at[route_ids].add(row_score.astype(jnp.float32), mode="drop")
        return (grad_acc, score_acc), (grad_gate_w, grad_up_w, grad_down_w)

    start_state = (jnp.zeros((token_count, tokens.shape[1]), jnp.float32),
                   jnp.zeros((route_count,), jnp.float32))
    final_state, weight_grads = lax.scan(per_expert, start_state, jnp.arange(EXPERTS, dtype=jnp.int32))
    grad_tokens = final_state[0].astype(jnp.bfloat16)
    grad_route_weight = final_state[1].reshape(token_count, top_count).astype(jnp.bfloat16)
    return (grad_tokens, grad_route_weight,
            weight_grads[0].astype(jnp.bfloat16),
            weight_grads[1].astype(jnp.bfloat16),
            weight_grads[2].astype(jnp.bfloat16))
```

```python
import jax
import jax.numpy as jnp
from jax import lax
from jax.sharding import PartitionSpec as P


def dot(a, b, dims):
    return lax.dot_general(a, b, (dims, ((), ())), preferred_element_type=jnp.float32)


def body(tokens, cotangent, routes, route_weight, w_gate, w_up, w_down):
    local = w_gate.shape[0]
    groups = lax.axis_size("expert")
    experts = local * groups
    rows = tokens.shape[0]
    ids = jnp.arange(experts, dtype=jnp.int32)
    chosen = routes[:, :, None] == ids[None, None, :]
    dense = jnp.sum(jnp.where(chosen, route_weight.astype(jnp.float32)[:, :, None], 0.0), axis=1)
    dense = dense.astype(jnp.bfloat16)
    x = lax.all_gather(tokens, "expert", tiled=True)
    g = lax.all_gather(cotangent, "expert", tiled=True)
    wt = lax.all_to_all(
        dense.reshape(rows, groups, local).transpose(1, 0, 2), "expert", 0, 0, tiled=True
    ).reshape(groups * rows, local)
    grad_rows = 0.0
    scores = []
    gg, gu, gd = [], [], []
    for l in range(local):
        w = wt[:, l : l + 1].astype(jnp.float32)
        a = dot(x, w_gate[l], ((1,), (0,)))
        u = dot(x, w_up[l], ((1,), (0,)))
        q = dot(g, w_down[l], ((1,), (0,)))
        s = jax.nn.sigmoid(a)
        silu = a * s
        h = silu * u
        scores.append(jnp.sum(h * q, axis=1))
        hw = (h * w).astype(jnp.bfloat16)
        wq = w * q
        dg = (wq * u * (s * (1.0 + a * (1.0 - s)))).astype(jnp.bfloat16)
        du = (wq * silu).astype(jnp.bfloat16)
        grad_rows = grad_rows + dot(dg, w_gate[l], ((1,), (1,))) + dot(du, w_up[l], ((1,), (1,)))
        gg.append(dot(x, dg, ((0,), (0,))))
        gu.append(dot(x, du, ((0,), (0,))))
        gd.append(dot(g, hw, ((0,), (0,))))
    grad_tokens = lax.psum_scatter(
        grad_rows.astype(jnp.bfloat16), "expert", scatter_dimension=0, tiled=True
    )
    score = jnp.stack(scores, axis=1).astype(jnp.bfloat16)
    back = lax.all_to_all(score.reshape(groups, rows, local), "expert", 0, 0, tiled=True)
    back = back.transpose(1, 0, 2).reshape(rows, experts).astype(jnp.float32)
    grw = jnp.sum(jnp.where(chosen, back[:, None, :], 0.0), axis=2)

    def over_dp(parts):
        return lax.psum_scatter(
            jnp.stack(parts).astype(jnp.bfloat16), "dp", scatter_dimension=1, tiled=True
        )

    return (
        grad_tokens.astype(jnp.bfloat16),
        grw.astype(jnp.bfloat16),
        over_dp(gg),
        over_dp(gu),
        over_dp(gd),
    )


def solution(mesh):
    return jax.shard_map(
        body,
        mesh=mesh,
        in_specs=(P(("dp", "expert"), None),) * 4 + (P("expert", None, None),) * 3,
        out_specs=(P(("dp", "expert"), None),) * 2 + (P("expert", "dp", None),) * 3,
        check_vma=False,
    )
```

```python
import functools

import jax
import jax.numpy as jnp
from jax import lax
from jax.experimental import pallas as pl
from jax.experimental.pallas import tpu as pltpu
from jax.sharding import PartitionSpec as P


def dot(a, b, dims):
    return lax.dot_general(a, b, (dims, ((), ())), preferred_element_type=jnp.float32)


def body(tokens, cotangent, routes, route_weight, w_gate, w_up, w_down):
    local = w_gate.shape[0]
    groups = lax.axis_size("expert")
    experts = local * groups
    rows = tokens.shape[0]
    ids = jnp.arange(experts, dtype=jnp.int32)
    chosen = routes[:, :, None] == ids[None, None, :]
    dense = jnp.sum(jnp.where(chosen, route_weight.astype(jnp.float32)[:, :, None], 0.0), axis=1)
    dense = dense.astype(jnp.bfloat16)
    x = lax.all_gather(tokens, "expert", tiled=True)
    g = lax.all_gather(cotangent, "expert", tiled=True)
    wt = lax.all_to_all(
        dense.reshape(rows, groups, local).transpose(1, 0, 2), "expert", 0, 0, tiled=True
    ).reshape(groups * rows, local)
    grad_rows = 0.0
    scores = []
    gg, gu, gd = [], [], []
    for l in range(local):
        w = wt[:, l : l + 1].astype(jnp.float32)
        a = dot(x, w_gate[l], ((1,), (0,)))
        u = dot(x, w_up[l], ((1,), (0,)))
        q = dot(g, w_down[l], ((1,), (0,)))
        s = jax.nn.sigmoid(a)
        silu = a * s
        h = silu * u
        scores.append(jnp.sum(h * q, axis=1))
        hw = (h * w).astype(jnp.bfloat16)
        wq = w * q
        dg = (wq * u * (s * (1.0 + a * (1.0 - s)))).astype(jnp.bfloat16)
        du = (wq * silu).astype(jnp.bfloat16)
        grad_rows = grad_rows + dot(dg, w_gate[l], ((1,), (1,))) + dot(du, w_up[l], ((1,), (1,)))
        gg.append(dot(x, dg, ((0,), (0,))))
        gu.append(dot(x, du, ((0,), (0,))))
        gd.append(dot(g, hw, ((0,), (0,))))
    grad_tokens = lax.psum_scatter(
        grad_rows.astype(jnp.bfloat16), "expert", scatter_dimension=0, tiled=True
    )
    score = jnp.stack(scores, axis=1).astype(jnp.bfloat16)
    back = lax.all_to_all(score.reshape(groups, rows, local), "expert", 0, 0, tiled=True)
    back = back.transpose(1, 0, 2).reshape(rows, experts).astype(jnp.float32)
    grw = jnp.sum(jnp.where(chosen, back[:, None, :], 0.0), axis=2)

    def over_dp(parts):
        return lax.psum_scatter(
            jnp.stack(parts).astype(jnp.bfloat16), "dp", scatter_dimension=1, tiled=True
        )

    return (
        grad_tokens.astype(jnp.bfloat16),
        grw.astype(jnp.bfloat16),
        over_dp(gg),
        over_dp(gu),
        over_dp(gd),
    )


F32 = jnp.float32
BF16 = jnp.bfloat16
UP, DOWN, ACROSS = 0, 1, 2


def visit(z, step, depth):
    mirrored = 2 * z >= depth
    base = jnp.where(mirrored, depth - 1 - z, z)
    half = (step + 1) // 2
    near = jnp.where(step % 2 == 1, base - half, base + half)
    order = jnp.where(step <= 2 * base, near, step)
    return jnp.where(mirrored, depth - 1 - order, order)


def kernel(
    depth,
    tokens,
    cotangent,
    routes,
    route_weight,
    w_gate,
    w_up,
    w_down,
    out_tokens,
    out_weight,
    out_gate,
    out_up,
    out_down,
    xg,
    gg,
    wg,
    wu,
    wd,
    dg,
    du,
    hw,
    part,
    part_in,
    red,
    red_in,
    core_out,
    core_in,
    y_out,
    y_in,
    acc,
    load_sem,
    send_x,
    send_g,
    recv_x,
    recv_g,
    send_p,
    recv_p,
    send_r,
    recv_r,
    send_c,
    recv_c,
    send_y,
    recv_y,
):
    rows, width = tokens.shape
    local, _, ff = w_gate.shape
    top = routes.shape[1]
    wide = local * ff
    full = width + 128
    slab = out_gate.shape[1]
    e = lax.axis_index("expert")
    dp = lax.axis_index("dp")
    z, x = e // 2, e % 2
    y, core = dp // 2, dp % 2
    partner = z * 2 + 1 - x
    core_peer = y * 2 + 1 - core
    y_peer = (1 - y) * 2 + core

    loads = []
    for i, (source, target) in enumerate(((w_gate, wg), (w_up, wu), (w_down, wd))):
        for l in range(local):
            loads.append(
                pltpu.make_async_copy(
                    source.at[l], target.at[:, pl.ds(l * ff, ff)], load_sem.at[i * local + l]
                )
            )
    for c in loads:
        c.start()

    barrier = pltpu.get_barrier_semaphore()
    pl.semaphore_signal(barrier, 1, device_id={"expert": partner}, device_id_type=pl.DeviceIdType.MESH)
    for k in range(1, depth):
        other = ((z + k) % depth) * 2 + x
        pl.semaphore_signal(barrier, 1, device_id={"expert": other}, device_id_type=pl.DeviceIdType.MESH)
    pl.semaphore_signal(barrier, 1, device_id={"dp": core_peer}, device_id_type=pl.DeviceIdType.MESH)
    pl.semaphore_signal(barrier, 1, device_id={"dp": y_peer}, device_id_type=pl.DeviceIdType.MESH)

    def block(i, n=rows):
        return pl.ds(pl.multiple_of(i * n, n), n)

    lane = lax.broadcasted_iota(jnp.int32, (rows, 128), 1)
    dense = jnp.zeros((rows, 128), F32)
    weights = route_weight[...].astype(F32)
    for k in range(top):
        dense = dense + jnp.where(routes[:, k : k + 1] == lane, weights[:, k : k + 1], 0.0)
    xg[block(e), pl.ds(0, width)] = tokens[...]
    xg[block(e), pl.ds(width, 128)] = dense.astype(BF16)
    gg[block(e), :] = cotangent[...]
    pl.semaphore_wait(barrier, depth + 2)

    def move(buf, send, recv, i, way, target):
        return pltpu.make_async_remote_copy(
            buf.at[block(i)],
            buf.at[block(i)],
            send.at[i * 3 + way],
            recv.at[i],
            device_id={"expert": target},
            device_id_type=pl.DeviceIdType.MESH,
        )

    pairs = ((xg, send_x, recv_x), (gg, send_g, recv_g))

    def up(p, i):
        return move(*p, i, UP, e + 2)

    def down(p, i):
        return move(*p, i, DOWN, e - 2)

    def across(p, i):
        return move(*p, i, ACROSS, partner)

    for p in pairs:

        @pl.when(z < depth - 1)
        def _():
            up(p, e).start()

        @pl.when(z > 0)
        def _():
            down(p, e).start()

        across(p, e).start()
    for c in loads:
        c.wait()

    column = lax.broadcasted_iota(jnp.int32, (128, wide), 1)
    owner = lax.broadcasted_iota(jnp.int32, (128, wide), 0) - e * local
    hit = jnp.zeros((128, wide), F32)
    for l in range(local):
        inside = (column >= l * ff) & (column < (l + 1) * ff) & (owner == l)
        hit = hit + jnp.where(inside, 1.0, 0.0)
    hit = hit.astype(BF16)

    def share(zz):
        return pltpu.make_async_remote_copy(
            part.at[block(zz * 2 + 1 - x)],
            part_in.at[block(zz)],
            send_p.at[zz],
            recv_p.at[zz],
            device_id={"expert": partner},
            device_id_type=pl.DeviceIdType.MESH,
        )

    def home(zz):
        return pltpu.make_async_remote_copy(
            red.at[block(zz)],
            red_in.at[block(z)],
            send_r.at[zz],
            recv_r.at[z],
            device_id={"expert": zz * 2 + x},
            device_id_type=pl.DeviceIdType.MESH,
        )

    def landed(zz):
        return pltpu.make_async_remote_copy(
            red.at[block(zz)],
            red_in.at[block(zz)],
            send_r.at[zz],
            recv_r.at[zz],
            device_id={"expert": zz * 2 + x},
            device_id_type=pl.DeviceIdType.MESH,
        )

    def reduce(zz):
        share(zz).wait_recv()
        total = part[block(zz * 2 + x), :].astype(F32) + part_in[block(zz), :].astype(F32)
        red[block(zz), :] = total.astype(BF16)

        @pl.when(zz != z)
        def _():
            home(zz).start()

    def work(zz):
        here = block(zz, 2 * rows)
        xs = xg[here, pl.ds(0, width)]
        ws = xg[here, pl.ds(width, 128)]
        gs = gg[here, :]
        score = jnp.zeros((2 * rows, 128), F32)
        cut = 256
        for f in range(0, wide, cut):
            cols = pl.ds(f, cut)
            pick = hit[:, f : f + cut]
            w = dot(ws, pick, ((1,), (0,)))
            a = dot(xs, wg[:, cols], ((1,), (0,)))
            u = dot(xs, wu[:, cols], ((1,), (0,)))
            q = dot(gs, wd[:, cols], ((1,), (0,)))
            s = 1.0 / (1.0 + jnp.exp(-a))
            silu = a * s
            h = silu * u
            score = score + dot((h * q).astype(BF16), pick, ((1,), (1,)))
            wq = w * q
            hw[here, cols] = (h * w).astype(BF16)
            dg[here, cols] = (wq * u * (s * (1.0 + a * (1.0 - s)))).astype(BF16)
            du[here, cols] = (wq * silu).astype(BF16)
        part[here, pl.ds(width, 128)] = score.astype(BF16)
        for d in range(0, width, 256):
            cols = pl.ds(d, 256)
            back = dot(dg[here, :], wg[cols, :], ((1,), (1,)))
            back = back + dot(du[here, :], wu[cols, :], ((1,), (1,)))
            part[here, cols] = back.astype(BF16)

    def step(s, carry):
        d = s + 1

        @pl.when(z - d >= 0)
        def _():
            i = e - 2 * d
            for p in pairs:
                up(p, i).wait_recv()

                @pl.when(z < depth - 1)
                def _():
                    up(p, i).start()

                across(p, i).start()

        @pl.when(z + d < depth)
        def _():
            i = e + 2 * d
            for p in pairs:
                down(p, i).wait_recv()

                @pl.when(z > 0)
                def _():
                    down(p, i).start()

                across(p, i).start()

        zz = visit(z, s, depth)
        for p in pairs:
            across(p, zz * 2 + 1 - x).wait_recv()
        work(zz)
        share(zz).start()

        @pl.when(s > 0)
        def _():
            reduce(visit(z, s - 1, depth))

        return carry

    lax.fori_loop(0, depth, step, 0)

    def slab_grads(c):
        cols = pl.ds(pl.multiple_of(c * slab, slab), slab)
        xt = xg[:, cols].T
        yield dot(xt, dg[...], ((1,), (0,)))
        yield dot(xt, du[...], ((1,), (0,)))
        yield dot(gg[:, cols].T, hw[...], ((1,), (0,)))

    def to_core(half, i):
        k = half * 3 + i
        return pltpu.make_async_remote_copy(
            core_out.at[k],
            core_in.at[k],
            send_c.at[k],
            recv_c.at[k],
            device_id={"dp": core_peer},
            device_id_type=pl.DeviceIdType.MESH,
        )

    def to_y(i):
        return pltpu.make_async_remote_copy(
            y_out.at[i],
            y_in.at[i],
            send_y.at[i],
            recv_y.at[i],
            device_id={"dp": y_peer},
            device_id_type=pl.DeviceIdType.MESH,
        )

    for i, g in enumerate(slab_grads((1 - y) * 2 + 1 - core)):
        core_out[i] = g.astype(BF16)
        to_core(0, i).start()
    reduce(visit(z, depth - 1, depth))
    for i, g in enumerate(slab_grads(y_peer)):
        acc[i] = g
        to_core(0, i).wait_recv()
        y_out[i] = (acc[i] + core_in[i].astype(F32)).astype(BF16)
        to_y(i).start()
    for i, g in enumerate(slab_grads(core_peer)):
        core_out[3 + i] = g.astype(BF16)
        to_core(1, i).start()
    for i, g in enumerate(slab_grads(dp)):
        acc[i] = g

    total = red[block(z), :].astype(F32)
    for k in range(1, depth):
        zz = (z + k) % depth
        landed(zz).wait_recv()
        total = total + red_in[block(zz), :].astype(F32)
    out_tokens[...] = total[:, :width].astype(BF16)
    scores = total[:, width:full]
    for k in range(top):
        mine = jnp.where(routes[:, k : k + 1] == lane, scores, 0.0)
        out_weight[:, k : k + 1] = jnp.sum(mine, axis=1, keepdims=True).astype(BF16)

    for i, out in enumerate((out_gate, out_up, out_down)):
        to_core(1, i).wait_recv()
        to_y(i).wait_recv()
        g = acc[i] + core_in[3 + i].astype(F32) + y_in[i].astype(F32)
        for l in range(local):
            out[l] = g[:, l * ff : (l + 1) * ff].astype(BF16)

    for i in range(3):
        to_core(0, i).wait_send()
        to_core(1, i).wait_send()
        to_y(i).wait_send()

    def drain(zz, carry):
        i = zz * 2 + x
        for p in pairs:

            @pl.when((zz <= z) & (z < depth - 1))
            def _():
                up(p, i).wait_send()

            @pl.when((zz >= z) & (z > 0))
            def _():
                down(p, i).wait_send()

            across(p, i).wait_send()
        share(zz).wait_send()

        @pl.when(zz != z)
        def _():
            home(zz).wait_send()

        return carry

    lax.fori_loop(0, depth, drain, 0)


def fused(tokens, cotangent, routes, route_weight, w_gate, w_up, w_down):
    rows, width = tokens.shape
    local, _, ff = w_gate.shape
    groups = lax.axis_size("expert")
    depth = groups // 2
    wide = local * ff
    slab = width // lax.axis_size("dp")
    every = rows * groups
    full = width + 128
    vmem = pl.BlockSpec(memory_space=pltpu.VMEM)
    hbm = pl.BlockSpec(memory_space=pl.ANY)
    dma = pltpu.SemaphoreType.DMA
    grad = jax.ShapeDtypeStruct((local, slab, ff), BF16)
    return pl.pallas_call(
        functools.partial(kernel, depth),
        out_shape=(
            jax.ShapeDtypeStruct(tokens.shape, BF16),
            jax.ShapeDtypeStruct(routes.shape, BF16),
            grad,
            grad,
            grad,
        ),
        in_specs=[vmem] * 4 + [hbm] * 3,
        out_specs=[vmem] * 5,
        scratch_shapes=[
            pltpu.VMEM((every, full), BF16),
            pltpu.VMEM((every, width), BF16),
            pltpu.VMEM((width, wide), BF16),
            pltpu.VMEM((width, wide), BF16),
            pltpu.VMEM((width, wide), BF16),
            pltpu.VMEM((every, wide), BF16),
            pltpu.VMEM((every, wide), BF16),
            pltpu.VMEM((every, wide), BF16),
            pltpu.VMEM((every, full), BF16),
            pltpu.VMEM((depth * rows, full), BF16),
            pltpu.VMEM((depth * rows, full), BF16),
            pltpu.VMEM((depth * rows, full), BF16),
            pltpu.VMEM((6, slab, wide), BF16),
            pltpu.VMEM((6, slab, wide), BF16),
            pltpu.VMEM((3, slab, wide), BF16),
            pltpu.VMEM((3, slab, wide), BF16),
            pltpu.VMEM((3, slab, wide), F32),
            dma((3 * local,)),
            dma((3 * groups,)),
            dma((3 * groups,)),
            dma((groups,)),
            dma((groups,)),
            dma((depth,)),
            dma((depth,)),
            dma((depth,)),
            dma((depth,)),
            dma((6,)),
            dma((6,)),
            dma((3,)),
            dma((3,)),
        ],
        compiler_params=pltpu.CompilerParams(
            collective_id=0, has_side_effects=True, vmem_limit_bytes=52 * 1024 * 1024
        ),
        cost_estimate=pl.CostEstimate(
            flops=16 * every * width * wide,
            bytes_accessed=6 * width * wide,
            transcendentals=every * wide,
        ),
    )(tokens, cotangent, routes, route_weight, w_gate, w_up, w_down)


def solution(mesh):
    small = mesh.shape["expert"] == 8 and mesh.shape["dp"] == 4
    return jax.shard_map(
        fused if small else body,
        mesh=mesh,
        in_specs=(P(("dp", "expert"), None),) * 4 + (P("expert", None, None),) * 3,
        out_specs=(P(("dp", "expert"), None),) * 2 + (P("expert", "dp", None),) * 3,
        check_vma=False,
    )
```

```python
import functools

import jax
import jax.numpy as jnp
from jax import lax
from jax.experimental import pallas as pl
from jax.experimental.pallas import tpu as pltpu
from jax.sharding import PartitionSpec as P


def dot(a, b, dims):
    return lax.dot_general(a, b, (dims, ((), ())), preferred_element_type=jnp.float32)


def body(tokens, cotangent, routes, route_weight, w_gate, w_up, w_down):
    local = w_gate.shape[0]
    groups = lax.axis_size("expert")
    experts = local * groups
    rows = tokens.shape[0]
    ids = jnp.arange(experts, dtype=jnp.int32)
    chosen = routes[:, :, None] == ids[None, None, :]
    dense = jnp.sum(jnp.where(chosen, route_weight.astype(jnp.float32)[:, :, None], 0.0), axis=1)
    dense = dense.astype(jnp.bfloat16)
    x = lax.all_gather(tokens, "expert", tiled=True)
    g = lax.all_gather(cotangent, "expert", tiled=True)
    wt = lax.all_to_all(
        dense.reshape(rows, groups, local).transpose(1, 0, 2), "expert", 0, 0, tiled=True
    ).reshape(groups * rows, local)
    grad_rows = 0.0
    scores = []
    gg, gu, gd = [], [], []
    for l in range(local):
        w = wt[:, l : l + 1].astype(jnp.float32)
        a = dot(x, w_gate[l], ((1,), (0,)))
        u = dot(x, w_up[l], ((1,), (0,)))
        q = dot(g, w_down[l], ((1,), (0,)))
        s = jax.nn.sigmoid(a)
        silu = a * s
        h = silu * u
        scores.append(jnp.sum(h * q, axis=1))
        hw = (h * w).astype(jnp.bfloat16)
        wq = w * q
        dg = (wq * u * (s * (1.0 + a * (1.0 - s)))).astype(jnp.bfloat16)
        du = (wq * silu).astype(jnp.bfloat16)
        grad_rows = grad_rows + dot(dg, w_gate[l], ((1,), (1,))) + dot(du, w_up[l], ((1,), (1,)))
        gg.append(dot(x, dg, ((0,), (0,))))
        gu.append(dot(x, du, ((0,), (0,))))
        gd.append(dot(g, hw, ((0,), (0,))))
    grad_tokens = lax.psum_scatter(
        grad_rows.astype(jnp.bfloat16), "expert", scatter_dimension=0, tiled=True
    )
    score = jnp.stack(scores, axis=1).astype(jnp.bfloat16)
    back = lax.all_to_all(score.reshape(groups, rows, local), "expert", 0, 0, tiled=True)
    back = back.transpose(1, 0, 2).reshape(rows, experts).astype(jnp.float32)
    grw = jnp.sum(jnp.where(chosen, back[:, None, :], 0.0), axis=2)

    def over_dp(parts):
        return lax.psum_scatter(
            jnp.stack(parts).astype(jnp.bfloat16), "dp", scatter_dimension=1, tiled=True
        )

    return (
        grad_tokens.astype(jnp.bfloat16),
        grw.astype(jnp.bfloat16),
        over_dp(gg),
        over_dp(gu),
        over_dp(gd),
    )


F32 = jnp.float32
BF16 = jnp.bfloat16
UP, DOWN, ACROSS = 0, 1, 2


def visit(z, step, depth):
    mirrored = 2 * z >= depth
    base = jnp.where(mirrored, depth - 1 - z, z)
    half = (step + 1) // 2
    near = jnp.where(step % 2 == 1, base - half, base + half)
    order = jnp.where(step <= 2 * base, near, step)
    return jnp.where(mirrored, depth - 1 - order, order)


def kernel(
    depth,
    tokens,
    cotangent,
    routes,
    route_weight,
    w_gate,
    w_up,
    w_down,
    out_tokens,
    out_weight,
    out_gate,
    out_up,
    out_down,
    xg,
    gg,
    wg,
    wu,
    wd,
    dg,
    du,
    hw,
    part,
    part_in,
    red,
    red_in,
    core_out,
    core_in,
    y_out,
    y_in,
    acc,
    load_sem,
    send_x,
    send_g,
    recv_x,
    recv_g,
    send_p,
    recv_p,
    send_r,
    recv_r,
    send_c,
    recv_c,
    send_y,
    recv_y,
):
    rows, width = tokens.shape
    local, _, ff = w_gate.shape
    top = routes.shape[0]
    wide = local * ff
    full = width + 128
    slab = out_gate.shape[1]
    e = lax.axis_index("expert")
    dp = lax.axis_index("dp")
    z, x = e // 2, e % 2
    y, core = dp // 2, dp % 2
    partner = z * 2 + 1 - x
    core_peer = y * 2 + 1 - core
    y_peer = (1 - y) * 2 + core

    loads = []
    for i, (source, target) in enumerate(((w_gate, wg), (w_up, wu), (w_down, wd))):
        for l in range(local):
            loads.append(
                pltpu.make_async_copy(
                    source.at[l], target.at[:, pl.ds(l * ff, ff)], load_sem.at[i * local + l]
                )
            )
    for c in loads:
        c.start()

    barrier = pltpu.get_barrier_semaphore()
    pl.semaphore_signal(barrier, 1, device_id={"expert": partner}, device_id_type=pl.DeviceIdType.MESH)
    for k in range(1, depth):
        other = ((z + k) % depth) * 2 + x
        pl.semaphore_signal(barrier, 1, device_id={"expert": other}, device_id_type=pl.DeviceIdType.MESH)
    pl.semaphore_signal(barrier, 1, device_id={"dp": core_peer}, device_id_type=pl.DeviceIdType.MESH)
    pl.semaphore_signal(barrier, 1, device_id={"dp": y_peer}, device_id_type=pl.DeviceIdType.MESH)

    def block(i, n=rows):
        return pl.ds(pl.multiple_of(i * n, n), n)

    expert = lax.broadcasted_iota(jnp.int32, (128, rows), 0)
    dense = jnp.zeros((128, rows), F32)
    weights = route_weight[...].astype(F32)
    for k in range(top):
        dense = dense + jnp.where(routes[k : k + 1, :] == expert, weights[k : k + 1, :], 0.0)
    dense = dense.T
    xg[block(e), pl.ds(0, width)] = tokens[...]
    xg[block(e), pl.ds(width, 128)] = dense.astype(BF16)
    gg[block(e), :] = cotangent[...]
    pl.semaphore_wait(barrier, depth + 2)

    early = 3 * rows // 8
    pieces = (
        (xg, send_x, recv_x, 0, 0, early),
        (xg, send_x, recv_x, 1, early, rows - early),
        (gg, send_g, recv_g, 0, 0, rows // 2),
        (gg, send_g, recv_g, 1, rows // 2, rows // 2),
    )

    def move(piece, i, way, target):
        buf, send, recv, k, first, count = piece
        where = pl.ds(pl.multiple_of(i * rows + first, 16), count)
        return pltpu.make_async_remote_copy(
            buf.at[where],
            buf.at[where],
            send.at[(i * 2 + k) * 3 + way],
            recv.at[i * 2 + k],
            device_id={"expert": target},
            device_id_type=pl.DeviceIdType.MESH,
        )

    def up(p, i):
        return move(p, i, UP, e + 2)

    def down(p, i):
        return move(p, i, DOWN, e - 2)

    def across(p, i):
        return move(p, i, ACROSS, partner)

    def along(p, i):
        @pl.when(z < depth - 1)
        def _():
            up(p, i).start()

        @pl.when(z > 0)
        def _():
            down(p, i).start()

    for p in pieces:
        across(p, e).start()
        along(p, e)
        if p is pieces[1]:
            across(pieces[0], partner).wait_recv()
            along(pieces[0], partner)
    for c in loads:
        c.wait()

    column = lax.broadcasted_iota(jnp.int32, (128, wide), 1)
    owner = lax.broadcasted_iota(jnp.int32, (128, wide), 0) - e * local
    hit = jnp.zeros((128, wide), F32)
    for l in range(local):
        inside = (column >= l * ff) & (column < (l + 1) * ff) & (owner == l)
        hit = hit + jnp.where(inside, 1.0, 0.0)
    hit = hit.astype(BF16)

    def share(zz):
        return pltpu.make_async_remote_copy(
            part.at[block(zz * 2 + 1 - x)],
            part_in.at[block(zz)],
            send_p.at[zz],
            recv_p.at[zz],
            device_id={"expert": partner},
            device_id_type=pl.DeviceIdType.MESH,
        )

    def home(zz):
        return pltpu.make_async_remote_copy(
            red.at[block(zz)],
            red_in.at[block(z)],
            send_r.at[zz],
            recv_r.at[z],
            device_id={"expert": zz * 2 + x},
            device_id_type=pl.DeviceIdType.MESH,
        )

    def landed(zz):
        return pltpu.make_async_remote_copy(
            red.at[block(zz)],
            red_in.at[block(zz)],
            send_r.at[zz],
            recv_r.at[zz],
            device_id={"expert": zz * 2 + x},
            device_id_type=pl.DeviceIdType.MESH,
        )

    def reduce(zz):
        share(zz).wait_recv()
        total = part[block(zz * 2 + x), :].astype(F32) + part_in[block(zz), :].astype(F32)
        red[block(zz), :] = total.astype(BF16)

        @pl.when(zz != z)
        def _():
            home(zz).start()

    def work(zz):
        here = block(zz, 2 * rows)
        xs = xg[here, pl.ds(0, width)]
        ws = xg[here, pl.ds(width, 128)]
        gs = gg[here, :]
        score = jnp.zeros((2 * rows, 128), F32)
        cut = 256
        for f in range(0, wide, cut):
            cols = pl.ds(f, cut)
            pick = hit[:, f : f + cut]
            w = dot(ws, pick, ((1,), (0,)))
            a = dot(xs, wg[:, cols], ((1,), (0,)))
            u = dot(xs, wu[:, cols], ((1,), (0,)))
            q = dot(gs, wd[:, cols], ((1,), (0,)))
            s = 1.0 / (1.0 + jnp.exp(-a))
            silu = a * s
            h = silu * u
            score = score + dot((h * q).astype(BF16), pick, ((1,), (1,)))
            wq = w * q
            hw[here, cols] = (h * w).astype(BF16)
            dg[here, cols] = (wq * u * (s * (1.0 + a * (1.0 - s)))).astype(BF16)
            du[here, cols] = (wq * silu).astype(BF16)
        part[here, pl.ds(width, 128)] = score.astype(BF16)
        for d in range(0, width, 256):
            cols = pl.ds(d, 256)
            back = dot(dg[here, :], wg[cols, :], ((1,), (1,)))
            back = back + dot(du[here, :], wu[cols, :], ((1,), (1,)))
            part[here, cols] = back.astype(BF16)

    def step(s, carry):
        d = s + 1

        def pass_on(p, i, below):
            if below:
                up(p, i).wait_recv()

                @pl.when(z < depth - 1)
                def _():
                    up(p, i).start()

            else:
                down(p, i).wait_recv()

                @pl.when(z > 0)
                def _():
                    down(p, i).start()

        for p in pieces:

            @pl.when(z - d >= 0)
            def _():
                pass_on(p, e - 2 * d, True)
                if p is pieces[0]:
                    pass_on(p, partner - 2 * d, True)
                else:
                    across(p, e - 2 * d).start()

            @pl.when(z + d < depth)
            def _():
                pass_on(p, e + 2 * d, False)
                if p is pieces[0]:
                    pass_on(p, partner + 2 * d, False)
                else:
                    across(p, e + 2 * d).start()

        zz = visit(z, s, depth)
        for p in pieces[1:]:
            across(p, zz * 2 + 1 - x).wait_recv()
        work(zz)

        return carry

    lax.fori_loop(0, depth, step, 0)

    def slab_grads(c):
        cols = pl.ds(pl.multiple_of(c * slab, slab), slab)
        xt = xg[:, cols].T
        yield dot(xt, dg[...], ((1,), (0,)))
        yield dot(xt, du[...], ((1,), (0,)))
        yield dot(gg[:, cols].T, hw[...], ((1,), (0,)))

    def to_core(half, i):
        k = half * 3 + i
        return pltpu.make_async_remote_copy(
            core_out.at[k],
            core_in.at[k],
            send_c.at[k],
            recv_c.at[k],
            device_id={"dp": core_peer},
            device_id_type=pl.DeviceIdType.MESH,
        )

    def to_y(i):
        return pltpu.make_async_remote_copy(
            y_out.at[i],
            y_in.at[i],
            send_y.at[i],
            recv_y.at[i],
            device_id={"dp": y_peer},
            device_id_type=pl.DeviceIdType.MESH,
        )

    def ahead(k):
        return visit(z, depth - 1 - k, depth)

    for k in range(depth):
        share(ahead(k)).start()
    for i, g in enumerate(slab_grads((1 - y) * 2 + 1 - core)):
        core_out[i] = g.astype(BF16)
        to_core(0, i).start()
    for i, g in enumerate(slab_grads(y_peer)):
        acc[i] = g
        to_core(0, i).wait_recv()
        y_out[i] = (acc[i] + core_in[i].astype(F32)).astype(BF16)
        to_y(i).start()
    reduce(ahead(0))
    for i, g in enumerate(slab_grads(core_peer)):
        core_out[3 + i] = g.astype(BF16)
        to_core(1, i).start()
    reduce(ahead(1))
    for i, g in enumerate(slab_grads(dp)):
        acc[i] = g
    for k in range(2, depth):
        reduce(ahead(k))

    total = red[block(z), :].astype(F32)
    for k in range(1, depth):
        zz = (z + k) % depth
        landed(zz).wait_recv()
        total = total + red_in[block(zz), :].astype(F32)
    out_tokens[...] = total[:, :width].astype(BF16)
    scores = total[:, width:full].T
    picked = []
    for k in range(top):
        mine = jnp.where(routes[k : k + 1, :] == expert, scores, 0.0)
        picked.append(jnp.sum(mine, axis=0, keepdims=True))
    out_weight[...] = jnp.concatenate(picked, axis=0).astype(BF16)

    for i, out in enumerate((out_gate, out_up, out_down)):
        to_core(1, i).wait_recv()
        to_y(i).wait_recv()
        g = acc[i] + core_in[3 + i].astype(F32) + y_in[i].astype(F32)
        for l in range(local):
            out[l] = g[:, l * ff : (l + 1) * ff].astype(BF16)

    across(pieces[0], e).wait_send()
    for i in range(3):
        to_core(0, i).wait_send()
        to_core(1, i).wait_send()
        to_y(i).wait_send()

    def drain(zz, carry):
        i = zz * 2 + x
        def sent(p, i):
            @pl.when((zz <= z) & (z < depth - 1))
            def _():
                up(p, i).wait_send()

            @pl.when((zz >= z) & (z > 0))
            def _():
                down(p, i).wait_send()

        for p in pieces:
            sent(p, i)
        sent(pieces[0], zz * 2 + 1 - x)
        for p in pieces[1:]:
            across(p, i).wait_send()
        share(zz).wait_send()

        @pl.when(zz != z)
        def _():
            home(zz).wait_send()

        return carry

    lax.fori_loop(0, depth, drain, 0)


def fused(tokens, cotangent, routes, route_weight, w_gate, w_up, w_down):
    rows, width = tokens.shape
    local, _, ff = w_gate.shape
    groups = lax.axis_size("expert")
    depth = groups // 2
    wide = local * ff
    slab = width // lax.axis_size("dp")
    every = rows * groups
    full = width + 128
    vmem = pl.BlockSpec(memory_space=pltpu.VMEM)
    hbm = pl.BlockSpec(memory_space=pl.ANY)
    dma = pltpu.SemaphoreType.DMA
    grad = jax.ShapeDtypeStruct((local, slab, ff), BF16)
    outs = pl.pallas_call(
        functools.partial(kernel, depth),
        out_shape=(
            jax.ShapeDtypeStruct(tokens.shape, BF16),
            jax.ShapeDtypeStruct(routes.shape[::-1], BF16),
            grad,
            grad,
            grad,
        ),
        in_specs=[vmem] * 4 + [hbm] * 3,
        out_specs=[vmem] * 5,
        scratch_shapes=[
            pltpu.VMEM((every, full), BF16),
            pltpu.VMEM((every, width), BF16),
            pltpu.VMEM((width, wide), BF16),
            pltpu.VMEM((width, wide), BF16),
            pltpu.VMEM((width, wide), BF16),
            pltpu.VMEM((every, wide), BF16),
            pltpu.VMEM((every, wide), BF16),
            pltpu.VMEM((every, wide), BF16),
            pltpu.VMEM((every, full), BF16),
            pltpu.VMEM((depth * rows, full), BF16),
            pltpu.VMEM((depth * rows, full), BF16),
            pltpu.VMEM((depth * rows, full), BF16),
            pltpu.VMEM((6, slab, wide), BF16),
            pltpu.VMEM((6, slab, wide), BF16),
            pltpu.VMEM((3, slab, wide), BF16),
            pltpu.VMEM((3, slab, wide), BF16),
            pltpu.VMEM((3, slab, wide), F32),
            dma((3 * local,)),
            dma((6 * groups,)),
            dma((6 * groups,)),
            dma((2 * groups,)),
            dma((2 * groups,)),
            dma((depth,)),
            dma((depth,)),
            dma((depth,)),
            dma((depth,)),
            dma((6,)),
            dma((6,)),
            dma((3,)),
            dma((3,)),
        ],
        compiler_params=pltpu.CompilerParams(
            collective_id=0, has_side_effects=True, vmem_limit_bytes=52 * 1024 * 1024
        ),
        cost_estimate=pl.CostEstimate(
            flops=16 * every * width * wide,
            bytes_accessed=6 * width * wide,
            transcendentals=every * wide,
        ),
    )(tokens, cotangent, routes.T, route_weight.T, w_gate, w_up, w_down)
    return outs[0], outs[1].T, *outs[2:]


def solution(mesh):
    small = mesh.shape["expert"] == 8 and mesh.shape["dp"] == 4
    return jax.shard_map(
        fused if small else body,
        mesh=mesh,
        in_specs=(P(("dp", "expert"), None),) * 4 + (P("expert", None, None),) * 3,
        out_specs=(P(("dp", "expert"), None),) * 2 + (P("expert", "dp", None),) * 3,
        check_vma=False,
    )
```

```python
import functools

import jax
import jax.numpy as jnp
from jax import lax
from jax.experimental import pallas as pl
from jax.experimental.pallas import tpu as pltpu
from jax.sharding import PartitionSpec as P


def dot(a, b, dims):
    return lax.dot_general(a, b, (dims, ((), ())), preferred_element_type=jnp.float32)


def body(tokens, cotangent, routes, route_weight, w_gate, w_up, w_down):
    local = w_gate.shape[0]
    groups = lax.axis_size("expert")
    experts = local * groups
    rows = tokens.shape[0]
    ids = jnp.arange(experts, dtype=jnp.int32)
    chosen = routes[:, :, None] == ids[None, None, :]
    dense = jnp.sum(jnp.where(chosen, route_weight.astype(jnp.float32)[:, :, None], 0.0), axis=1)
    dense = dense.astype(jnp.bfloat16)
    x = lax.all_gather(tokens, "expert", tiled=True)
    g = lax.all_gather(cotangent, "expert", tiled=True)
    wt = lax.all_to_all(
        dense.reshape(rows, groups, local).transpose(1, 0, 2), "expert", 0, 0, tiled=True
    ).reshape(groups * rows, local)
    grad_rows = 0.0
    scores = []
    gg, gu, gd = [], [], []
    for l in range(local):
        w = wt[:, l : l + 1].astype(jnp.float32)
        a = dot(x, w_gate[l], ((1,), (0,)))
        u = dot(x, w_up[l], ((1,), (0,)))
        q = dot(g, w_down[l], ((1,), (0,)))
        s = jax.nn.sigmoid(a)
        silu = a * s
        h = silu * u
        scores.append(jnp.sum(h * q, axis=1))
        hw = (h * w).astype(jnp.bfloat16)
        wq = w * q
        dg = (wq * u * (s * (1.0 + a * (1.0 - s)))).astype(jnp.bfloat16)
        du = (wq * silu).astype(jnp.bfloat16)
        grad_rows = grad_rows + dot(dg, w_gate[l], ((1,), (1,))) + dot(du, w_up[l], ((1,), (1,)))
        gg.append(dot(x, dg, ((0,), (0,))))
        gu.append(dot(x, du, ((0,), (0,))))
        gd.append(dot(g, hw, ((0,), (0,))))
    grad_tokens = lax.psum_scatter(
        grad_rows.astype(jnp.bfloat16), "expert", scatter_dimension=0, tiled=True
    )
    score = jnp.stack(scores, axis=1).astype(jnp.bfloat16)
    back = lax.all_to_all(score.reshape(groups, rows, local), "expert", 0, 0, tiled=True)
    back = back.transpose(1, 0, 2).reshape(rows, experts).astype(jnp.float32)
    grw = jnp.sum(jnp.where(chosen, back[:, None, :], 0.0), axis=2)

    def over_dp(parts):
        return lax.psum_scatter(
            jnp.stack(parts).astype(jnp.bfloat16), "dp", scatter_dimension=1, tiled=True
        )

    return (
        grad_tokens.astype(jnp.bfloat16),
        grw.astype(jnp.bfloat16),
        over_dp(gg),
        over_dp(gu),
        over_dp(gd),
    )


F32 = jnp.float32
BF16 = jnp.bfloat16
UP, DOWN, ACROSS = 0, 1, 2


def visit(z, step, depth):
    mirrored = 2 * z >= depth
    base = jnp.where(mirrored, depth - 1 - z, z)
    half = (step + 1) // 2
    near = jnp.where(step % 2 == 1, base - half, base + half)
    order = jnp.where(step <= 2 * base, near, step)
    return jnp.where(mirrored, depth - 1 - order, order)


def kernel(
    depth,
    tokens,
    cotangent,
    routes,
    route_weight,
    w_gate,
    w_up,
    w_down,
    out_tokens,
    out_weight,
    out_gate,
    out_up,
    out_down,
    xg,
    gg,
    wg,
    wu,
    wd,
    dg,
    du,
    hw,
    part,
    part_in,
    red,
    red_in,
    core_out,
    core_in,
    y_out,
    y_in,
    acc,
    load_sem,
    send_x,
    send_g,
    recv_x,
    recv_g,
    send_p,
    recv_p,
    send_r,
    recv_r,
    send_c,
    recv_c,
    send_y,
    recv_y,
):
    rows, width = tokens.shape
    local, _, ff = w_gate.shape
    top = routes.shape[0]
    wide = local * ff
    full = width + 128
    slab = out_gate.shape[1]
    e = lax.axis_index("expert")
    dp = lax.axis_index("dp")
    z, x = e // 2, e % 2
    y, core = dp // 2, dp % 2
    partner = z * 2 + 1 - x
    core_peer = y * 2 + 1 - core
    y_peer = (1 - y) * 2 + core

    loads = []
    for i, (source, target) in enumerate(((w_gate, wg), (w_up, wu), (w_down, wd))):
        for l in range(local):
            loads.append(
                pltpu.make_async_copy(
                    source.at[l], target.at[:, pl.ds(l * ff, ff)], load_sem.at[i * local + l]
                )
            )
    for c in loads:
        c.start()

    barrier = pltpu.get_barrier_semaphore()
    pl.semaphore_signal(barrier, 1, device_id={"expert": partner}, device_id_type=pl.DeviceIdType.MESH)
    for k in range(1, depth):
        other = ((z + k) % depth) * 2 + x
        pl.semaphore_signal(barrier, 1, device_id={"expert": other}, device_id_type=pl.DeviceIdType.MESH)
    pl.semaphore_signal(barrier, 1, device_id={"dp": core_peer}, device_id_type=pl.DeviceIdType.MESH)
    pl.semaphore_signal(barrier, 1, device_id={"dp": y_peer}, device_id_type=pl.DeviceIdType.MESH)

    def block(i, n=rows):
        return pl.ds(pl.multiple_of(i * n, n), n)

    expert = lax.broadcasted_iota(jnp.int32, (128, rows), 0)
    dense = jnp.zeros((128, rows), F32)
    weights = route_weight[...].astype(F32)
    for k in range(top):
        dense = dense + jnp.where(routes[k : k + 1, :] == expert, weights[k : k + 1, :], 0.0)
    dense = dense.T
    xg[block(e), pl.ds(0, width)] = tokens[...]
    xg[block(e), pl.ds(width, 128)] = dense.astype(BF16)
    gg[block(e), :] = cotangent[...]
    pl.semaphore_wait(barrier, depth + 2)

    early = rows // 2
    pieces = (
        (xg, send_x, recv_x, 0, 0, early),
        (xg, send_x, recv_x, 1, early, rows - early),
        (gg, send_g, recv_g, 0, 0, rows // 2),
        (gg, send_g, recv_g, 1, rows // 2, rows // 2),
    )

    def move(piece, i, way, target):
        buf, send, recv, k, first, count = piece
        where = pl.ds(pl.multiple_of(i * rows + first, 16), count)
        return pltpu.make_async_remote_copy(
            buf.at[where],
            buf.at[where],
            send.at[(i * 2 + k) * 3 + way],
            recv.at[i * 2 + k],
            device_id={"expert": target},
            device_id_type=pl.DeviceIdType.MESH,
        )

    def up(p, i):
        return move(p, i, UP, e + 2)

    def down(p, i):
        return move(p, i, DOWN, e - 2)

    def across(p, i):
        return move(p, i, ACROSS, partner)

    def along(p, i):
        @pl.when(z < depth - 1)
        def _():
            up(p, i).start()

        @pl.when(z > 0)
        def _():
            down(p, i).start()

    for p in pieces:
        across(p, e).start()
        along(p, e)
        if p is pieces[1]:
            across(pieces[0], partner).wait_recv()
            along(pieces[0], partner)
    for c in loads:
        c.wait()

    column = lax.broadcasted_iota(jnp.int32, (128, wide), 1)
    owner = lax.broadcasted_iota(jnp.int32, (128, wide), 0) - e * local
    hit = jnp.zeros((128, wide), F32)
    for l in range(local):
        inside = (column >= l * ff) & (column < (l + 1) * ff) & (owner == l)
        hit = hit + jnp.where(inside, 1.0, 0.0)
    hit = hit.astype(BF16)

    def share(zz):
        return pltpu.make_async_remote_copy(
            part.at[block(zz * 2 + 1 - x)],
            part_in.at[block(zz)],
            send_p.at[zz],
            recv_p.at[zz],
            device_id={"expert": partner},
            device_id_type=pl.DeviceIdType.MESH,
        )

    def home(zz):
        return pltpu.make_async_remote_copy(
            red.at[block(zz)],
            red_in.at[block(z)],
            send_r.at[zz],
            recv_r.at[z],
            device_id={"expert": zz * 2 + x},
            device_id_type=pl.DeviceIdType.MESH,
        )

    def landed(zz):
        return pltpu.make_async_remote_copy(
            red.at[block(zz)],
            red_in.at[block(zz)],
            send_r.at[zz],
            recv_r.at[zz],
            device_id={"expert": zz * 2 + x},
            device_id_type=pl.DeviceIdType.MESH,
        )

    def reduce(zz):
        share(zz).wait_recv()
        total = part[block(zz * 2 + x), :].astype(F32) + part_in[block(zz), :].astype(F32)
        red[block(zz), :] = total.astype(BF16)

        @pl.when(zz != z)
        def _():
            home(zz).start()

    def work(zz):
        here = block(zz, 2 * rows)
        xs = xg[here, pl.ds(0, width)]
        ws = xg[here, pl.ds(width, 128)]
        gs = gg[here, :]
        score = jnp.zeros((2 * rows, 128), F32)
        cut = 256
        for f in range(0, wide, cut):
            cols = pl.ds(f, cut)
            pick = hit[:, f : f + cut]
            w = dot(ws, pick, ((1,), (0,)))
            a = dot(xs, wg[:, cols], ((1,), (0,)))
            u = dot(xs, wu[:, cols], ((1,), (0,)))
            q = dot(gs, wd[:, cols], ((1,), (0,)))
            s = 1.0 / (1.0 + jnp.exp(-a))
            silu = a * s
            h = silu * u
            score = score + dot((h * q).astype(BF16), pick, ((1,), (1,)))
            wq = w * q
            hw[here, cols] = (h * w).astype(BF16)
            dg[here, cols] = (wq * u * (s * (1.0 + a * (1.0 - s)))).astype(BF16)
            du[here, cols] = (wq * silu).astype(BF16)
        part[here, pl.ds(width, 128)] = score.astype(BF16)
        for d in range(0, width, 256):
            cols = pl.ds(d, 256)
            back = dot(dg[here, :], wg[cols, :], ((1,), (1,)))
            back = back + dot(du[here, :], wu[cols, :], ((1,), (1,)))
            part[here, cols] = back.astype(BF16)

    def step(s, carry):
        d = s + 1

        def pass_on(p, i, below):
            if below:
                up(p, i).wait_recv()

                @pl.when(z < depth - 1)
                def _():
                    up(p, i).start()

            else:
                down(p, i).wait_recv()

                @pl.when(z > 0)
                def _():
                    down(p, i).start()

        for p in pieces:

            @pl.when(z - d >= 0)
            def _():
                pass_on(p, e - 2 * d, True)
                if p is pieces[0]:
                    pass_on(p, partner - 2 * d, True)
                else:
                    across(p, e - 2 * d).start()

            @pl.when(z + d < depth)
            def _():
                pass_on(p, e + 2 * d, False)
                if p is pieces[0]:
                    pass_on(p, partner + 2 * d, False)
                else:
                    across(p, e + 2 * d).start()

        zz = visit(z, s, depth)
        for p in pieces[1:]:
            across(p, zz * 2 + 1 - x).wait_recv()
        work(zz)

        @pl.when(s == 0)
        def _():
            share(zz).start()

        return carry

    lax.fori_loop(0, depth, step, 0)

    def slab_grads(c):
        cols = pl.ds(pl.multiple_of(c * slab, slab), slab)
        xt = xg[:, cols].T
        yield dot(xt, dg[...], ((1,), (0,)))
        yield dot(xt, du[...], ((1,), (0,)))
        yield dot(gg[:, cols].T, hw[...], ((1,), (0,)))

    def to_core(half, i):
        k = half * 3 + i
        return pltpu.make_async_remote_copy(
            core_out.at[k],
            core_in.at[k],
            send_c.at[k],
            recv_c.at[k],
            device_id={"dp": core_peer},
            device_id_type=pl.DeviceIdType.MESH,
        )

    def to_y(i):
        return pltpu.make_async_remote_copy(
            y_out.at[i],
            y_in.at[i],
            send_y.at[i],
            recv_y.at[i],
            device_id={"dp": y_peer},
            device_id_type=pl.DeviceIdType.MESH,
        )

    def ahead(k):
        return visit(z, depth - 1 - k, depth)

    for k in range(depth - 1):
        share(ahead(k)).start()
    for i, g in enumerate(slab_grads((1 - y) * 2 + 1 - core)):
        core_out[i] = g.astype(BF16)
        to_core(0, i).start()
    for i, g in enumerate(slab_grads(y_peer)):
        acc[i] = g
        to_core(0, i).wait_recv()
        y_out[i] = (acc[i] + core_in[i].astype(F32)).astype(BF16)
        to_y(i).start()
    reduce(ahead(0))
    for i, g in enumerate(slab_grads(core_peer)):
        core_out[3 + i] = g.astype(BF16)
        to_core(1, i).start()
    reduce(ahead(1))
    for i, g in enumerate(slab_grads(dp)):
        acc[i] = g
    for k in range(2, depth):
        reduce(ahead(k))

    total = red[block(z), :].astype(F32)
    for k in range(1, depth):
        zz = (z + k) % depth
        landed(zz).wait_recv()
        total = total + red_in[block(zz), :].astype(F32)
    out_tokens[...] = total[:, :width].astype(BF16)
    scores = total[:, width:full].T
    picked = []
    for k in range(top):
        mine = jnp.where(routes[k : k + 1, :] == expert, scores, 0.0)
        picked.append(jnp.sum(mine, axis=0, keepdims=True))
    out_weight[...] = jnp.concatenate(picked, axis=0).astype(BF16)

    for i, out in enumerate((out_gate, out_up, out_down)):
        to_core(1, i).wait_recv()
        to_y(i).wait_recv()
        g = acc[i] + core_in[3 + i].astype(F32) + y_in[i].astype(F32)
        for l in range(local):
            out[l] = g[:, l * ff : (l + 1) * ff].astype(BF16)

    across(pieces[0], e).wait_send()
    for i in range(3):
        to_core(0, i).wait_send()
        to_core(1, i).wait_send()
        to_y(i).wait_send()

    def drain(zz, carry):
        i = zz * 2 + x
        def sent(p, i):
            @pl.when((zz <= z) & (z < depth - 1))
            def _():
                up(p, i).wait_send()

            @pl.when((zz >= z) & (z > 0))
            def _():
                down(p, i).wait_send()

        for p in pieces:
            sent(p, i)
        sent(pieces[0], zz * 2 + 1 - x)
        for p in pieces[1:]:
            across(p, i).wait_send()
        share(zz).wait_send()

        @pl.when(zz != z)
        def _():
            home(zz).wait_send()

        return carry

    lax.fori_loop(0, depth, drain, 0)


def fused(tokens, cotangent, routes, route_weight, w_gate, w_up, w_down):
    rows, width = tokens.shape
    local, _, ff = w_gate.shape
    groups = lax.axis_size("expert")
    depth = groups // 2
    wide = local * ff
    slab = width // lax.axis_size("dp")
    every = rows * groups
    full = width + 128
    vmem = pl.BlockSpec(memory_space=pltpu.VMEM)
    hbm = pl.BlockSpec(memory_space=pl.ANY)
    dma = pltpu.SemaphoreType.DMA
    grad = jax.ShapeDtypeStruct((local, slab, ff), BF16)
    outs = pl.pallas_call(
        functools.partial(kernel, depth),
        out_shape=(
            jax.ShapeDtypeStruct(tokens.shape, BF16),
            jax.ShapeDtypeStruct(routes.shape[::-1], BF16),
            grad,
            grad,
            grad,
        ),
        in_specs=[vmem] * 4 + [hbm] * 3,
        out_specs=[vmem] * 5,
        scratch_shapes=[
            pltpu.VMEM((every, full), BF16),
            pltpu.VMEM((every, width), BF16),
            pltpu.VMEM((width, wide), BF16),
            pltpu.VMEM((width, wide), BF16),
            pltpu.VMEM((width, wide), BF16),
            pltpu.VMEM((every, wide), BF16),
            pltpu.VMEM((every, wide), BF16),
            pltpu.VMEM((every, wide), BF16),
            pltpu.VMEM((every, full), BF16),
            pltpu.VMEM((depth * rows, full), BF16),
            pltpu.VMEM((depth * rows, full), BF16),
            pltpu.VMEM((depth * rows, full), BF16),
            pltpu.VMEM((6, slab, wide), BF16),
            pltpu.VMEM((6, slab, wide), BF16),
            pltpu.VMEM((3, slab, wide), BF16),
            pltpu.VMEM((3, slab, wide), BF16),
            pltpu.VMEM((3, slab, wide), F32),
            dma((3 * local,)),
            dma((6 * groups,)),
            dma((6 * groups,)),
            dma((2 * groups,)),
            dma((2 * groups,)),
            dma((depth,)),
            dma((depth,)),
            dma((depth,)),
            dma((depth,)),
            dma((6,)),
            dma((6,)),
            dma((3,)),
            dma((3,)),
        ],
        compiler_params=pltpu.CompilerParams(
            collective_id=0, has_side_effects=True, vmem_limit_bytes=52 * 1024 * 1024
        ),
        cost_estimate=pl.CostEstimate(
            flops=16 * every * width * wide,
            bytes_accessed=6 * width * wide,
            transcendentals=every * wide,
        ),
    )(tokens, cotangent, routes.T, route_weight.T, w_gate, w_up, w_down)
    return outs[0], outs[1].T, *outs[2:]


def solution(mesh):
    small = mesh.shape["expert"] == 8 and mesh.shape["dp"] == 4
    return jax.shard_map(
        fused if small else body,
        mesh=mesh,
        in_specs=(P(("dp", "expert"), None),) * 4 + (P("expert", None, None),) * 3,
        out_specs=(P(("dp", "expert"), None),) * 2 + (P("expert", "dp", None),) * 3,
        check_vma=False,
    )
```
